256 devices in a mesh: dom: 16 (over y_hi, x, core), orient: 16 (over z, y_lo).
Axes of the slice: x: 4, y: 4 (y_hi: 2, y_lo: 2; y = y_hi * 2 + y_lo), z: 8, core: 2. Of those that a mesh axis runs over, the one named last changes fastest.
Arguments:
- images: bfloat16 [2816, 32768], P('dom'), may hold values from -128 to 128
- ctf_table: bfloat16 [8, 32768], replicated, may hold values from 0.29882812 to 1.5
- group_ids: int32 [2816], P('dom'), may hold values from 0 to 7
- projections: bfloat16 [2048, 32768], P('orient', 'dom'), may hold values from -4 to 4
- log_prior: float32 [2048], P('orient'), may hold values from -2 to 3
Outputs:
- numerator: bfloat16 [32768, 2048], P('dom', 'orient')
The draws below stay inside these ranges and needn't reach their ends.
All inputs are finite; a program needn't handle non-finite values.
Results may differ from the reference program's by a relative error of at most 0.017.
Values may be sent and summed in bfloat16 or wider, within the bound.
A program may use at most 128 MiB of HBM per device.

```python
import math
import jax
import jax.numpy as jnp
from jax import lax

PIX = 32768
ROWS = 2048
GROUPS = 8
B_DEV = 176
PARTICLES = 2816
N_DOM = 16


def projection_rows(key, rows):
    base = jax.random.fold_in(key, 101)

    def one_row(row):
        return jnp.clip(jax.random.normal(jax.random.fold_in(base, row), (PIX,), jnp.float32), -4.0, 4.0)
    return jax.vmap(one_row)(rows)


def draw_projections(key, part):
    rows = jnp.arange(ROWS, dtype=jnp.int32)
    return projection_rows(key, rows).astype(jnp.bfloat16)


def place_aligned(shared, key, base):
    key_pick, key_first, key_second = jax.random.split(key, 3)
    count = PARTICLES // 16
    chosen = jax.random.permutation(key_pick, PARTICLES)[:count]
    first = jax.random.randint(key_first, (count,), 0, ROWS)
    second = (first + jax.random.randint(key_second, (count,), 1, ROWS)) % ROWS
    target = 150.0 + 50.0 * (jnp.arange(count) % 4).astype(jnp.float32)
    strength = (target / math.sqrt(PIX) + 0.45) / 0.9
    aligned = strength[:, None] * (projection_rows(shared, first) + projection_rows(shared, second))
    return base.at[chosen].set(jnp.clip(aligned, -128.0, 128.0))


def draw_images(key, part):
    shared = key
    key = jax.random.fold_in(key, 7)
    key_base = jax.random.fold_in(key, 1)
    key_align = jax.random.fold_in(key, 2)
    base = jnp.clip(jax.random.normal(key_base, (PARTICLES, PIX), jnp.float32), -6.0, 6.0)
    base = place_aligned(shared, key_align, base)
    return base.astype(jnp.bfloat16)


def draw_log_prior(key, part):
    key = jax.random.fold_in(key, 13)
    position = jnp.arange(ROWS, dtype=jnp.float32) / ROWS
    values = math.log(3.0) * position - 0.5 + 0.9 * jnp.clip(jax.random.normal(key, (ROWS,), jnp.float32), -2.5, 2.5)
    return jnp.clip(values, -2.0, 3.0)


def with_ends(values, key, least, high):
    place = [jax.random.randint(jax.random.fold_in(key, axis), (), 0, length) for axis, length in enumerate(values.shape)]
    main_axis = values.shape.index(max(values.shape))
    neighbour = place[:main_axis] + [(place[main_axis] + 1) % values.shape[main_axis]] + place[main_axis + 1:]
    return values.at[tuple(place)].set(least).at[tuple(neighbour)].set(high)


def setup_inputs(seed: int = 0) -> dict:
    key_list = jax.random.split(jax.random.key(seed), 6)
    return {
        "images": draw_images(jax.random.fold_in(key_list[5], 71), 0),
        "ctf_table": jnp.clip(jax.random.uniform(key_list[1], (GROUPS, PIX), jnp.float32, 0.29882812, 1.5), 0.29882812, 1.5).astype(jnp.bfloat16),
        "group_ids": with_ends(jax.random.randint(key_list[2], (PARTICLES,), 0, GROUPS), jax.random.fold_in(key_list[2], 1), 0, GROUPS - 1).astype(jnp.int32),
        "projections": draw_projections(jax.random.fold_in(key_list[5], 71), 0),
        "log_prior": draw_log_prior(jax.random.fold_in(key_list[5], 71), 0),
    }


def reference(images, ctf_table, group_ids, projections, log_prior):
    highest = lax.Precision.HIGHEST
    onehot = (group_ids[:, None] == jnp.arange(GROUPS, dtype=jnp.int32)[None, :]).astype(jnp.float32)
    ctf_wide = ctf_table.astype(jnp.float32)
    ctf_rows = jnp.dot(onehot, ctf_wide, precision=highest)
    weighted = (ctf_rows * images.astype(jnp.float32)).astype(jnp.bfloat16)
    proj_sq = projections.astype(jnp.float32) ** 2
    norms = lax.dot_general(ctf_wide * ctf_wide, proj_sq, (((1,), (1,)), ((), ())), precision=highest)
    dots = lax.dot_general(weighted, projections, (((1,), (1,)), ((), ())), preferred_element_type=jnp.float32)
    lookup = jnp.dot(onehot, norms, precision=highest)
    scores = (dots - 0.5 * lookup) * (1.0 / jnp.sqrt(jnp.float32(PIX))) + log_prior[None, :]
    top = lax.optimization_barrier(jnp.max(scores, axis=1))
    expo = jnp.exp(scores - top[:, None])
    total = lax.optimization_barrier(jnp.sum(expo, axis=1))
    weights = (expo / total[:, None]).astype(jnp.bfloat16)
    image_blocks = weighted.reshape(N_DOM, B_DEV, PIX)
    weight_blocks = weights.reshape(N_DOM, B_DEV, ROWS)

    def add_block(acc, pair):
        block_images, block_weights = pair
        term = lax.dot_general(block_images, block_weights, (((0,), (0,)), ((), ())), preferred_element_type=jnp.float32)
        rounded = lax.optimization_barrier(term.astype(jnp.bfloat16))
        return (acc + rounded.astype(jnp.float32), None)
    start = jnp.zeros((PIX, ROWS), jnp.float32)
    numerator, unused = lax.scan(add_block, start, (image_blocks, weight_blocks))
    return numerator.astype(jnp.bfloat16)
```

```python
import functools

import jax
import jax.numpy as jnp
import numpy as np
from jax import lax
from jax.experimental import pallas as pl
from jax.experimental.pallas import tpu as pltpu
from jax.sharding import PartitionSpec as P

BF = jnp.bfloat16
F32 = jnp.float32
MESH = pl.DeviceIdType.MESH
NX, NZ = 4, 8
NQ = 4
LOW, HIGH = (0, 1), (2, 3)
QS = (0, 1, 2, 3)
MIXED = (0, 2, 1, 3)
PAD = 256
ORDER = ((0, 0), (0, 3), (0, 1), (1, 0), (0, 2), (1, 2), (1, 3), (1, 1))
FAR, DIAG3, DIAG1, OWN3, OWN1, ACROSS, HALF = range(7)


def nt(a, b):
    return lax.dot_general(a, b, (((1,), (1,)), ((), ())), preferred_element_type=F32)


def nn(a, b):
    return jnp.dot(a, b, preferred_element_type=F32)


def split3(v):
    a = v.astype(BF)
    r = v - a.astype(F32)
    b = r.astype(BF)
    return a, b, (r - b.astype(F32)).astype(BF)


def kernel(
    images,
    ctf,
    gids,
    proj,
    prior,
    out,
    raw,
    weighted,
    stage,
    blocks,
    ctfv,
    ctf_sq,
    hot,
    hot_t,
    acc,
    norm,
    xsend,
    xrecv,
    stat,
    wts,
    part,
    rx,
    raw_sem,
    loc_sem,
    g_send,
    g_recv,
    w_send,
    w_recv,
    hot_sem,
    x_send,
    x_recv,
    st_send,
    st_recv,
    wt_send,
    wt_recv,
    r_send,
    r_recv,
):
    n_loc, pix = images.shape
    n_rows, width = proj.shape
    step = width // NQ
    scale = float(np.float32(1.0) / np.sqrt(np.float32(pix)))
    dom, ori = lax.axis_index("dom"), lax.axis_index("orient")
    yh, x, core = dom // (2 * NX), lax.rem(dom // 2, NX), lax.rem(dom, 2)
    z, yl = ori // 2, lax.rem(ori, 2)

    def device(yh_, x_, core_, yl_):
        return {"dom": (yh_ * NX + x_) * 2 + core_, "orient": z * 2 + yl_}

    xp = device(yh, lax.rem(x + 1, NX), core, yl)
    xm = device(yh, lax.rem(x + NX - 1, NX), core, yl)
    yp = device(1 - yh, x, core, 1 - yl)
    sib = device(yh, x, 1 - core, yl)
    near = device(yh, x, core, 1 - yl)
    diag = device(yh, x, 1 - core, 1 - yl)

    def peer(k):
        return {"dom": dom, "orient": lax.rem(ori + k, 2 * NZ)}

    def pixel_block(s, j, core_):
        yh_ = yh if s == 0 else 1 - yh
        return (yh_ * NX + lax.rem(x + j, NX)) * 2 + core_

    jobs = [(s, j, own) for s, j in ORDER for own in (0, 1)]
    n_raw = raw.shape[0]

    def raw_copy(i):
        s, j, own = jobs[i]
        d = pixel_block(s, j, core if own else 1 - core)
        start = pl.multiple_of(d * width, width)
        return pltpu.make_async_copy(
            images.at[:, pl.ds(start, width)], raw.at[i % n_raw], raw_sem.at[i % n_raw]
        )

    ctf_copy = pltpu.make_async_copy(ctf, ctfv, loc_sem.at[NQ])
    ctf_copy.start()
    for i in range(n_raw):
        raw_copy(i).start()
    own_copies = [
        pltpu.make_async_copy(
            proj.at[:, pl.ds(q * step, step)], blocks.at[0, 0, q], loc_sem.at[q]
        )
        for q in QS
    ]
    for copy in own_copies:
        copy.start()

    barrier = pltpu.get_barrier_semaphore()
    for who in (xp, xm, yp, sib, diag):
        pl.semaphore_signal(barrier, inc=1, device_id=who, device_id_type=MESH)

    @pl.loop(1, 2 * NZ)
    def _(k):
        pl.semaphore_signal(barrier, inc=1, device_id=peer(k), device_id_type=MESH)

    pl.semaphore_wait(barrier, 5 + 2 * NZ - 1)

    links = (xp, xm, yp)
    counts = [0, 0, 0]
    sent = []

    def gather(link, src, s, j, q):
        copy = pltpu.make_async_remote_copy(
            src_ref=src,
            dst_ref=blocks.at[s, j, q],
            send_sem=g_send.at[link, counts[link]],
            recv_sem=g_recv.at[s, j, q],
            device_id=links[link],
            device_id_type=MESH,
        )
        counts[link] += 1
        copy.start()
        sent.append(copy)

    def arrived(s, j, q):
        pltpu.make_async_remote_copy(
            src_ref=blocks.at[s, j, q],
            dst_ref=blocks.at[s, j, q],
            send_sem=g_send.at[0, 0],
            recv_sem=g_recv.at[s, j, q],
            device_id=xp,
            device_id_type=MESH,
        ).wait_recv()

    for a, b in zip(LOW + HIGH, HIGH + LOW):
        gather(0, proj.at[:, pl.ds(a * step, step)], 0, 3, a)
        gather(1, proj.at[:, pl.ds(b * step, step)], 0, 1, b)
        gather(2, proj.at[:, pl.ds(a * step, step)], 1, 0, a)

    group = lax.broadcasted_iota(jnp.int32, (n_rows, n_loc), 0)
    hot_full = jnp.where(group == gids[...], 1.0, 0.0)
    acc[0, 0] = jnp.zeros((n_rows, PAD), F32)
    acc[0, 0, :, :n_loc] = hot_full
    hot_t[...] = jnp.transpose(acc[0, 0])[:n_loc, :].astype(BF)
    twice = jnp.concatenate([acc[0, 0, :8, :], acc[0, 0, :8, :]], axis=0)
    hot[0] = twice.astype(BF)
    hot_copy = pltpu.make_async_remote_copy(
        src_ref=hot.at[0],
        dst_ref=hot.at[1],
        send_sem=hot_sem.at[0],
        recv_sem=hot_sem.at[1],
        device_id=sib,
        device_id_type=MESH,
    )
    hot_copy.start()
    acc[...] = jnp.zeros(acc.shape, F32)
    norm[...] = jnp.zeros(norm.shape, F32)
    ctf_copy.wait()

    def weigh(i):
        s, j, own = jobs[i]
        d = pixel_block(s, j, core if own else 1 - core)
        dst = weighted.at[0, s, j] if own else stage.at[s, j]
        raw_copy(i).wait()
        tile = 256

        @pl.loop(0, width // tile)
        def _(t):
            here = pl.ds(pl.multiple_of(t * tile, tile), tile)
            there = pl.ds(pl.multiple_of(d * width + t * tile, tile), tile)
            table = ctfv[:, there]
            rows = nn(hot_t[:, :8], table)
            dst[:, here] = (rows * raw[i % n_raw, :, here].astype(F32)).astype(BF)
            if own:
                wide = table.astype(F32)
                square = wide * wide
                high = square.astype(BF).astype(F32)
                both = jnp.concatenate([high, square - high], axis=0)
                ctf_sq[s, j, :, here] = both.astype(BF)

        if i + n_raw < len(jobs):
            raw_copy(i + n_raw).start()
        if not own:
            copy = weighted_copy(s, j)
            copy.start()

    def weighted_copy(s, j):
        return pltpu.make_async_remote_copy(
            src_ref=stage.at[s, j],
            dst_ref=weighted.at[1, s, j],
            send_sem=w_send.at[s, j],
            recv_sem=w_recv.at[s, j],
            device_id=sib,
            device_id_type=MESH,
        )

    def score(s, j, q):
        here = pl.ds(pl.multiple_of(q * step, step), step)
        block = blocks[s, j, q]
        for nb in (0, 1):
            acc[s, nb, :, :n_loc] += nt(block, weighted[nb, s, j, :, here])
        wide = block.astype(F32)
        square = wide * wide
        high = square.astype(BF)
        low = (square - high.astype(F32)).astype(BF)
        table = ctf_sq[s, j, :, here]
        norm[s] += nt(high, table) + nt(low, table)

    def score_block(s, j):
        @pl.loop(0, NQ)
        def _(q):
            score(s, j, q)

    for i in range(8):
        weigh(i)
    for a, b in zip(LOW, HIGH):
        arrived(0, 3, a)
        gather(0, blocks.at[0, 3, a], 0, 2, a)
        arrived(0, 1, b)
        gather(1, blocks.at[0, 1, b], 0, 2, b)
    for i in range(8, 16):
        weigh(i)
    for q in QS:
        arrived(1, 0, q)
        gather(0, blocks.at[1, 0, q], 1, 3, q)
        gather(1, blocks.at[1, 0, q], 1, 1, q)
    for copy in own_copies:
        copy.wait()
    weighted_copy(0, 0).wait_recv()
    score_block(0, 0)
    for a, b in zip(LOW, HIGH):
        arrived(0, 3, b)
        arrived(0, 1, a)
    weighted_copy(0, 3).wait_recv()
    score_block(0, 3)
    weighted_copy(0, 1).wait_recv()
    score_block(0, 1)
    for q in MIXED:
        arrived(0, 2, q)
        gather(2, blocks.at[0, 2, q], 1, 2, q)
    weighted_copy(0, 2).wait_recv()
    score_block(0, 2)

    hot_copy.wait()

    def partial_scores(s, nb):
        a, b, c = split3(norm[s])
        look = nn(a, hot[nb]) + nn(b, hot[nb]) + nn(c, hot[nb])
        return (acc[s, nb] - 0.5 * look) * scale

    def exchange(i, who):
        return pltpu.make_async_remote_copy(
            src_ref=xsend.at[i],
            dst_ref=xrecv.at[i],
            send_sem=x_send.at[i],
            recv_sem=x_recv.at[i],
            device_id=who,
            device_id_type=MESH,
        )

    prior_rows = jnp.transpose(jnp.broadcast_to(prior[...], (n_rows, n_rows)))[:, :1]
    xsend[0] = partial_scores(0, 0) + prior_rows
    xsend[1] = partial_scores(0, 1)
    exchange(0, near).start()
    exchange(1, diag).start()

    weighted_copy(1, 0).wait_recv()
    score_block(1, 0)
    for j in (2, 3, 1):
        weighted_copy(1, j).wait_recv()
    for a, q in zip(MIXED, QS):
        arrived(1, 2, a)
        score(1, 2, a)
        arrived(1, 3, q)
        score(1, 3, q)
        arrived(1, 1, q)
        score(1, 1, q)

    xsend[2] = partial_scores(1, 1)
    exchange(2, sib).start()
    mine = partial_scores(1, 0)
    exchange(0, near).wait_recv()
    exchange(1, diag).wait_recv()
    mine += xrecv[0] + xrecv[1]
    exchange(2, sib).wait_recv()
    scores = mine + xrecv[2]

    largest = jnp.max(scores, axis=0, keepdims=True)
    expo = jnp.exp(scores - largest)
    stat[0, 0:1] = largest
    stat[0, 1:2] = jnp.sum(expo, axis=0, keepdims=True)
    stat[0, 2:8] = jnp.zeros((6, PAD), F32)

    def stat_copy(k):
        return pltpu.make_async_remote_copy(
            src_ref=stat.at[0],
            dst_ref=stat.at[k],
            send_sem=st_send.at[k],
            recv_sem=st_recv.at[k],
            device_id=peer(k),
            device_id_type=MESH,
        )

    @pl.loop(1, 2 * NZ)
    def _(k):
        stat_copy(k).start()

    @pl.loop(1, 2 * NZ)
    def _(k):
        stat_copy(k).wait_recv()

    tops = stat[:, 0, :]
    top = jnp.max(tops, axis=0, keepdims=True)
    total = jnp.sum(stat[:, 1, :] * jnp.exp(tops - top), axis=0, keepdims=True)
    wts[1, 0] = (expo * (jnp.exp(largest - top) / total)).astype(BF)

    def weight_copy(i):
        s, nb, who = ((1, 1, sib), (0, 0, near), (0, 1, diag))[i]
        return pltpu.make_async_remote_copy(
            src_ref=wts.at[1, 0],
            dst_ref=wts.at[s, nb],
            send_sem=wt_send.at[i],
            recv_sem=wt_recv.at[i],
            device_id=who,
            device_id_type=MESH,
        )

    for i in range(3):
        weight_copy(i).start()

    counts2 = [0, 0, 0]

    def here(q):
        return pl.ds(q * step, step)

    def sums(s, j, q):
        return nn(wts[s, 0, :, :n_loc], weighted[0, s, j, :, here(q)]) + nn(
            wts[s, 1, :, :n_loc], weighted[1, s, j, :, here(q)]
        )

    def landed(kind, q):
        pltpu.make_async_remote_copy(
            src_ref=rx.at[kind, q],
            dst_ref=rx.at[kind, q],
            send_sem=r_send.at[0, 0],
            recv_sem=r_recv.at[kind, q],
            device_id=xp,
            device_id_type=MESH,
        ).wait_recv()
        return rx[kind, q].astype(F32)

    def scatter(link, kind, s, j, q, *added):
        for k in added:
            pass
        total_ = sums(s, j, q)
        for k in added:
            total_ = total_ + landed(k, q)
        part[s, j, q] = total_.astype(BF)
        copy = pltpu.make_async_remote_copy(
            src_ref=part.at[s, j, q],
            dst_ref=rx.at[kind, q],
            send_sem=r_send.at[link, counts2[link]],
            recv_sem=r_recv.at[kind, q],
            device_id=links[link],
            device_id_type=MESH,
        )
        counts2[link] += 1
        copy.start()
        sent.append(copy)

    weight_copy(0).wait_recv()
    for a, q in zip(MIXED, QS):
        scatter(2, FAR, 1, 2, a)
        scatter(0, DIAG3, 1, 1, q)
        scatter(1, DIAG1, 1, 3, q)
    weight_copy(1).wait_recv()
    weight_copy(2).wait_recv()
    for i, (a, b) in enumerate(zip(LOW, HIGH)):
        scatter(1, HALF, 0, 2, a, FAR)
        scatter(2, ACROSS, 1, 0, 2 * i, DIAG3, DIAG1)
        scatter(0, HALF, 0, 2, b, FAR)
        scatter(2, ACROSS, 1, 0, 2 * i + 1, DIAG3, DIAG1)
    for a, b in zip(LOW, HIGH):
        scatter(0, OWN3, 0, 1, a)
        scatter(1, OWN1, 0, 3, b)
    for a, b in zip(LOW, HIGH):
        scatter(0, OWN3, 0, 1, b, HALF)
        scatter(1, OWN1, 0, 3, a, HALF)
    for q in QS:
        total_ = sums(0, 0, q) + landed(ACROSS, q) + landed(OWN3, q) + landed(OWN1, q)
        out[here(q), :] = jnp.transpose(total_).astype(BF)

    for copy in sent:
        copy.wait_send()
    for s, j in ORDER:
        weighted_copy(s, j).wait_send()
    for i, who in enumerate((near, diag, sib)):
        exchange(i, who).wait_send()

    @pl.loop(1, 2 * NZ)
    def _(k):
        stat_copy(k).wait_send()

    for i in range(3):
        weight_copy(i).wait_send()


def body(images, ctf_table, group_ids, projections, log_prior):
    n_loc, pix = images.shape
    n_rows, width = projections.shape
    step = width // NQ
    dma = pltpu.SemaphoreType.DMA
    scratch = [
        pltpu.VMEM((4, n_loc, width), BF),
        pltpu.VMEM((2, 2, NX, n_loc, width), BF),
        pltpu.VMEM((2, NX, n_loc, width), BF),
        pltpu.VMEM((2, NX, NQ, n_rows, step), BF),
        pltpu.VMEM(ctf_table.shape, BF),
        pltpu.VMEM((2, NX, 16, width), BF),
        pltpu.VMEM((2, 16, PAD), BF),
        pltpu.VMEM((n_loc, n_rows), BF),
        pltpu.VMEM((2, 2, n_rows, PAD), F32),
        pltpu.VMEM((2, n_rows, 16), F32),
        pltpu.VMEM((3, n_rows, PAD), F32),
        pltpu.VMEM((3, n_rows, PAD), F32),
        pltpu.VMEM((2 * NZ, 8, PAD), F32),
        pltpu.VMEM((2, 2, n_rows, PAD), BF),
        pltpu.VMEM((2, NX, NQ, n_rows, step), BF),
        pltpu.VMEM((7, NQ, n_rows, step), BF),
        dma((4,)),
        dma((NQ + 1,)),
        dma((3, 3 * NQ)),
        dma((2, NX, NQ)),
        dma((2, NX)),
        dma((2, NX)),
        dma((2,)),
        dma((3,)),
        dma((3,)),
        dma((2 * NZ,)),
        dma((2 * NZ,)),
        dma((3,)),
        dma((3,)),
        dma((3, 3 * NQ)),
        dma((7, NQ)),
    ]
    vmem = pl.BlockSpec(memory_space=pltpu.VMEM)
    hbm = pl.BlockSpec(memory_space=pl.ANY)
    return pl.pallas_call(
        kernel,
        out_shape=jax.ShapeDtypeStruct((width, n_rows), BF),
        in_specs=[hbm, hbm, vmem, hbm, vmem],
        out_specs=vmem,
        scratch_shapes=scratch,
        compiler_params=pltpu.CompilerParams(
            collective_id=0, has_side_effects=True, vmem_limit_bytes=56 << 20
        ),
    )(images, ctf_table, group_ids.reshape(1, n_loc), projections, log_prior.reshape(1, n_rows))


def solution(mesh):
    placed = (P("dom", None), P(), P("dom"), P("orient", "dom"), P("orient"))
    return jax.shard_map(
        body, mesh=mesh, in_specs=placed, out_specs=P("dom", "orient"), check_vma=False
    )
```

```python
import functools

import jax
import jax.numpy as jnp
import numpy as np
from jax import lax
from jax.experimental import pallas as pl
from jax.experimental.pallas import tpu as pltpu
from jax.sharding import PartitionSpec as P

BF = jnp.bfloat16
F32 = jnp.float32
MESH = pl.DeviceIdType.MESH
NX, NZ = 4, 8
SHARES = (4, 4, 4, 2, 2)
LOW, HIGH, VIA = (0, 1), (2, 3, 4), 4
PIECES = (0, 1, 2, 3, 4)
MIXED = (0, 2, 1, 3, 4)
NQ = 4
PAD = 256
ORDER = ((0, 0), (0, 3), (0, 1), (1, 0), (0, 2), (1, 2), (1, 3), (1, 1))
FAR, DIAG3, DIAG1, OWN3, OWN1, ACROSS, HALF, VIA1, VIA3 = range(9)


def nt(a, b):
    return lax.dot_general(a, b, (((1,), (1,)), ((), ())), preferred_element_type=F32)


def nn(a, b):
    return jnp.dot(a, b, preferred_element_type=F32)


def split3(v):
    a = v.astype(BF)
    r = v - a.astype(F32)
    b = r.astype(BF)
    return a, b, (r - b.astype(F32)).astype(BF)


def kernel(
    images,
    ctf,
    gids,
    proj,
    prior,
    out,
    raw,
    weighted,
    stage,
    blocks,
    ctfv,
    ctf_sq,
    hot,
    hot_t,
    acc,
    norm,
    xsend,
    xrecv,
    stat,
    wts,
    part,
    rx,
    raw_sem,
    loc_sem,
    g_send,
    g_recv,
    w_send,
    w_recv,
    hot_sem,
    x_send,
    x_recv,
    st_send,
    st_recv,
    wt_send,
    wt_recv,
    r_send,
    r_recv,
):
    n_loc, pix = images.shape
    n_rows, width = proj.shape
    step = width // NQ

    def piece(p):
        return pl.ds(sum(SHARES[:p]) * width // 16, SHARES[p] * width // 16)

    scale = float(np.float32(1.0) / np.sqrt(np.float32(pix)))
    dom, ori = lax.axis_index("dom"), lax.axis_index("orient")
    yh, x, core = dom // (2 * NX), lax.rem(dom // 2, NX), lax.rem(dom, 2)
    z, yl = ori // 2, lax.rem(ori, 2)

    def device(yh_, x_, core_, yl_):
        return {"dom": (yh_ * NX + x_) * 2 + core_, "orient": z * 2 + yl_}

    xp = device(yh, lax.rem(x + 1, NX), core, yl)
    xm = device(yh, lax.rem(x + NX - 1, NX), core, yl)
    yp = device(1 - yh, x, core, 1 - yl)
    sib = device(yh, x, 1 - core, yl)
    near = device(yh, x, core, 1 - yl)
    diag = device(yh, x, 1 - core, 1 - yl)

    def peer(k):
        return {"dom": dom, "orient": lax.rem(ori + k, 2 * NZ)}

    def pixel_block(s, j, core_):
        yh_ = yh if s == 0 else 1 - yh
        return (yh_ * NX + lax.rem(x + j, NX)) * 2 + core_

    jobs = [(s, j, own) for s, j in ORDER for own in (0, 1)]
    n_raw = raw.shape[0]

    def raw_copy(i):
        s, j, own = jobs[i]
        d = pixel_block(s, j, core if own else 1 - core)
        start = pl.multiple_of(d * width, width)
        return pltpu.make_async_copy(
            images.at[:, pl.ds(start, width)], raw.at[i % n_raw], raw_sem.at[i % n_raw]
        )

    ctf_copy = pltpu.make_async_copy(ctf, ctfv, loc_sem.at[1])
    ctf_copy.start()
    for i in range(n_raw):
        raw_copy(i).start()
    own_copy = pltpu.make_async_copy(proj, blocks.at[0, 0], loc_sem.at[0])
    own_copy.start()

    barrier = pltpu.get_barrier_semaphore()
    for who in (xp, xm, yp, sib, diag):
        pl.semaphore_signal(barrier, inc=1, device_id=who, device_id_type=MESH)

    @pl.loop(1, 2 * NZ)
    def _(k):
        pl.semaphore_signal(barrier, inc=1, device_id=peer(k), device_id_type=MESH)

    pl.semaphore_wait(barrier, 5 + 2 * NZ - 1)

    links = (xp, xm, yp)
    counts = [0, 0, 0]
    sent = []

    def gather(link, src, s, j, p):
        copy = pltpu.make_async_remote_copy(
            src_ref=src.at[:, piece(p)],
            dst_ref=blocks.at[s, j, :, piece(p)],
            send_sem=g_send.at[link, counts[link]],
            recv_sem=g_recv.at[s, j, p],
            device_id=links[link],
            device_id_type=MESH,
        )
        counts[link] += 1
        copy.start()
        sent.append(copy)

    def arrived(s, j, p):
        here = blocks.at[s, j, :, piece(p)]
        pltpu.make_async_remote_copy(
            src_ref=here,
            dst_ref=here,
            send_sem=g_send.at[0, 0],
            recv_sem=g_recv.at[s, j, p],
            device_id=xp,
            device_id_type=MESH,
        ).wait_recv()

    for a, b in zip(LOW + HIGH, HIGH + LOW):
        gather(0, proj, 0, 3, a)
        gather(1, proj, 0, 1, b)
        gather(2, proj, 1, 0, a)

    group = lax.broadcasted_iota(jnp.int32, (n_rows, n_loc), 0)
    hot_full = jnp.where(group == gids[...], 1.0, 0.0)
    acc[0, 0] = jnp.zeros((n_rows, PAD), F32)
    acc[0, 0, :, :n_loc] = hot_full
    hot_t[...] = jnp.transpose(acc[0, 0])[:n_loc, :].astype(BF)
    twice = jnp.concatenate([acc[0, 0, :8, :], acc[0, 0, :8, :]], axis=0)
    hot[0] = twice.astype(BF)
    hot_copy = pltpu.make_async_remote_copy(
        src_ref=hot.at[0],
        dst_ref=hot.at[1],
        send_sem=hot_sem.at[0],
        recv_sem=hot_sem.at[1],
        device_id=sib,
        device_id_type=MESH,
    )
    hot_copy.start()
    acc[...] = jnp.zeros(acc.shape, F32)
    norm[...] = jnp.zeros(norm.shape, F32)
    ctf_copy.wait()

    def weigh(i):
        s, j, own = jobs[i]
        d = pixel_block(s, j, core if own else 1 - core)
        dst = weighted.at[0, s, j] if own else stage.at[s, j]
        raw_copy(i).wait()
        tile = 1024

        @pl.loop(0, width // tile)
        def _(t):
            here = pl.ds(pl.multiple_of(t * tile, tile), tile)
            there = pl.ds(pl.multiple_of(d * width + t * tile, tile), tile)
            table = ctfv[:, there]
            rows = nn(hot_t[:, :8], table)
            dst[:, here] = (rows * raw[i % n_raw, :, here].astype(F32)).astype(BF)
            if own:
                wide = table.astype(F32)
                square = wide * wide
                high = square.astype(BF).astype(F32)
                both = jnp.concatenate([high, square - high], axis=0)
                ctf_sq[s, j, :, here] = both.astype(BF)

        if i + n_raw < len(jobs):
            raw_copy(i + n_raw).start()
        if not own:
            copy = weighted_copy(s, j)
            copy.start()

    def weighted_copy(s, j):
        return pltpu.make_async_remote_copy(
            src_ref=stage.at[s, j],
            dst_ref=weighted.at[1, s, j],
            send_sem=w_send.at[s, j],
            recv_sem=w_recv.at[s, j],
            device_id=sib,
            device_id_type=MESH,
        )

    def score(s, j, here):
        block = blocks[s, j, :, here]
        for nb in (0, 1):
            acc[s, nb, :, :n_loc] += nt(block, weighted[nb, s, j, :, here])
        wide = block.astype(F32)
        square = wide * wide
        high = square.astype(BF)
        low = (square - high.astype(F32)).astype(BF)
        table = ctf_sq[s, j, :, here]
        norm[s] += nt(high, table) + nt(low, table)

    def score_block(s, j):
        @pl.loop(0, NQ)
        def _(q):
            score(s, j, pl.ds(pl.multiple_of(q * step, step), step))

    for i in range(8):
        weigh(i)
    for p in LOW:
        arrived(0, 3, p)
        gather(0, blocks.at[0, 3], 0, 2, p)
    for p in HIGH:
        arrived(0, 1, p)
        gather(1, blocks.at[0, 1], 0, 2, p)
    for i in range(8, 16):
        weigh(i)
    gather(2, blocks.at[0, 1], 1, 1, VIA)
    for p in PIECES:
        arrived(1, 0, p)
        if p != VIA:
            gather(0, blocks.at[1, 0], 1, 3, p)
            gather(1, blocks.at[1, 0], 1, 1, p)
    for p in HIGH:
        arrived(0, 3, p)
    gather(2, blocks.at[0, 3], 1, 3, VIA)
    for p in LOW:
        arrived(0, 1, p)
    own_copy.wait()
    weighted_copy(0, 0).wait_recv()
    score_block(0, 0)
    for p in MIXED[:2]:
        arrived(0, 2, p)
        gather(2, blocks.at[0, 2], 1, 2, p)
    weighted_copy(0, 3).wait_recv()
    score_block(0, 3)
    for p in MIXED[2:]:
        arrived(0, 2, p)
        gather(2, blocks.at[0, 2], 1, 2, p)
    weighted_copy(0, 1).wait_recv()
    score_block(0, 1)
    weighted_copy(0, 2).wait_recv()
    score_block(0, 2)

    hot_copy.wait()

    def partial_scores(s, nb):
        a, b, c = split3(norm[s])
        look = nn(a, hot[nb]) + nn(b, hot[nb]) + nn(c, hot[nb])
        return (acc[s, nb] - 0.5 * look) * scale

    def exchange(i, who):
        return pltpu.make_async_remote_copy(
            src_ref=xsend.at[i],
            dst_ref=xrecv.at[i],
            send_sem=x_send.at[i],
            recv_sem=x_recv.at[i],
            device_id=who,
            device_id_type=MESH,
        )

    prior_rows = jnp.transpose(jnp.broadcast_to(prior[...], (n_rows, n_rows)))[:, :1]
    xsend[0] = partial_scores(0, 0) + prior_rows
    xsend[1] = partial_scores(0, 1)
    exchange(0, near).start()
    exchange(1, diag).start()

    weighted_copy(1, 0).wait_recv()
    score_block(1, 0)
    for j in (2, 3, 1):
        weighted_copy(1, j).wait_recv()
    arrived(1, 1, VIA)
    score(1, 1, piece(VIA))
    arrived(1, 3, VIA)
    score(1, 3, piece(VIA))
    for a, p in zip(MIXED, PIECES):
        if p != VIA:
            arrived(1, 3, p)
            score(1, 3, piece(p))
            arrived(1, 1, p)
            score(1, 1, piece(p))
        arrived(1, 2, a)
        score(1, 2, piece(a))

    xsend[2] = partial_scores(1, 1)
    exchange(2, sib).start()
    mine = partial_scores(1, 0)
    exchange(0, near).wait_recv()
    exchange(1, diag).wait_recv()
    mine += xrecv[0] + xrecv[1]
    exchange(2, sib).wait_recv()
    scores = mine + xrecv[2]

    largest = jnp.max(scores, axis=0, keepdims=True)
    expo = jnp.exp(scores - largest)
    stat[0, :, :PAD] = largest
    stat[0, :, PAD:] = jnp.sum(expo, axis=0, keepdims=True)

    def stat_copy(k):
        return pltpu.make_async_remote_copy(
            src_ref=stat.at[0],
            dst_ref=stat.at[k],
            send_sem=st_send.at[k],
            recv_sem=st_recv.at[k],
            device_id=peer(k),
            device_id_type=MESH,
        )

    @pl.loop(1, 2 * NZ)
    def _(k):
        stat_copy(k).start()

    @pl.loop(1, 2 * NZ)
    def _(k):
        stat_copy(k).wait_recv()

    top, total = largest, stat[0, :, PAD:]
    for k in range(1, 2 * NZ):
        top = jnp.maximum(top, stat[k, :, :PAD])
    total = jnp.zeros_like(top)
    for k in range(2 * NZ):
        total += stat[k, :, PAD:] * jnp.exp(stat[k, :, :PAD] - top)
    wts[1, 0] = (expo * (jnp.exp(largest - top) / total)).astype(BF)

    def weight_copy(i):
        s, nb, who = ((1, 1, sib), (0, 0, near), (0, 1, diag))[i]
        return pltpu.make_async_remote_copy(
            src_ref=wts.at[1, 0],
            dst_ref=wts.at[s, nb],
            send_sem=wt_send.at[i],
            recv_sem=wt_recv.at[i],
            device_id=who,
            device_id_type=MESH,
        )

    for i in range(3):
        weight_copy(i).start()

    counts2 = [0, 0, 0]

    def sums(s, j, p):
        return nn(wts[s, 0, :, :n_loc], weighted[0, s, j, :, piece(p)]) + nn(
            wts[s, 1, :, :n_loc], weighted[1, s, j, :, piece(p)]
        )

    def landed(kind, p):
        here = rx.at[kind, :, piece(p)]
        pltpu.make_async_remote_copy(
            src_ref=here,
            dst_ref=here,
            send_sem=r_send.at[0, 0],
            recv_sem=r_recv.at[kind, p],
            device_id=xp,
            device_id_type=MESH,
        ).wait_recv()
        return rx[kind, :, piece(p)].astype(F32)

    def scatter(link, kind, s, j, p, *added):
        total_ = sums(s, j, p)
        for k in added:
            total_ = total_ + landed(k, p)
        part[s, j, :, piece(p)] = total_.astype(BF)
        copy = pltpu.make_async_remote_copy(
            src_ref=part.at[s, j, :, piece(p)],
            dst_ref=rx.at[kind, :, piece(p)],
            send_sem=r_send.at[link, counts2[link]],
            recv_sem=r_recv.at[kind, p],
            device_id=links[link],
            device_id_type=MESH,
        )
        counts2[link] += 1
        copy.start()
        sent.append(copy)

    weight_copy(0).wait_recv()
    for a, p in zip(MIXED, PIECES):
        scatter(2, FAR, 1, 2, a)
        if p != VIA:
            scatter(0, DIAG3, 1, 1, p)
            scatter(1, DIAG1, 1, 3, p)
    scatter(2, VIA3, 1, 3, VIA)
    scatter(2, VIA1, 1, 1, VIA)
    weight_copy(1).wait_recv()
    weight_copy(2).wait_recv()
    scatter(1, HALF, 0, 2, 0, FAR)
    scatter(2, ACROSS, 1, 0, 0, DIAG3, DIAG1)
    scatter(0, HALF, 0, 2, 2, FAR)
    scatter(2, ACROSS, 1, 0, 1, DIAG3, DIAG1)
    scatter(1, HALF, 0, 2, 1, FAR)
    scatter(2, ACROSS, 1, 0, 2, DIAG3, DIAG1)
    scatter(0, HALF, 0, 2, 3, FAR)
    scatter(2, ACROSS, 1, 0, 3, DIAG3, DIAG1)
    scatter(2, ACROSS, 1, 0, 4)
    scatter(0, HALF, 0, 2, 4, FAR)
    scatter(0, OWN3, 0, 1, 0)
    scatter(1, OWN1, 0, 3, 2)
    scatter(0, OWN3, 0, 1, 1)
    scatter(1, OWN1, 0, 3, 3)
    scatter(1, OWN1, 0, 3, 4, VIA3)
    scatter(1, OWN1, 0, 3, 0, HALF)
    scatter(0, OWN3, 0, 1, 2, HALF)
    scatter(1, OWN1, 0, 3, 1, HALF)
    scatter(0, OWN3, 0, 1, 3, HALF)
    scatter(0, OWN3, 0, 1, 4, HALF, VIA1)
    for p in (2, 3, 4, 0, 1):
        total_ = sums(0, 0, p) + landed(ACROSS, p) + landed(OWN3, p) + landed(OWN1, p)
        out[piece(p), :] = jnp.transpose(total_).astype(BF)

    for copy in sent:
        copy.wait_send()
    for s, j in ORDER:
        weighted_copy(s, j).wait_send()
    for i, who in enumerate((near, diag, sib)):
        exchange(i, who).wait_send()

    @pl.loop(1, 2 * NZ)
    def _(k):
        stat_copy(k).wait_send()

    for i in range(3):
        weight_copy(i).wait_send()


def body(images, ctf_table, group_ids, projections, log_prior):
    n_loc, pix = images.shape
    n_rows, width = projections.shape
    dma = pltpu.SemaphoreType.DMA
    scratch = [
        pltpu.VMEM((4, n_loc, width), BF),
        pltpu.VMEM((2, 2, NX, n_loc, width), BF),
        pltpu.VMEM((2, NX, n_loc, width), BF),
        pltpu.VMEM((2, NX, n_rows, width), BF),
        pltpu.VMEM(ctf_table.shape, BF),
        pltpu.VMEM((2, NX, 16, width), BF),
        pltpu.VMEM((2, 16, PAD), BF),
        pltpu.VMEM((n_loc, n_rows), BF),
        pltpu.VMEM((2, 2, n_rows, PAD), F32),
        pltpu.VMEM((2, n_rows, 16), F32),
        pltpu.VMEM((3, n_rows, PAD), F32),
        pltpu.VMEM((3, n_rows, PAD), F32),
        pltpu.VMEM((2 * NZ, 1, 2 * PAD), F32),
        pltpu.VMEM((2, 2, n_rows, PAD), BF),
        pltpu.VMEM((2, NX, n_rows, width), BF),
        pltpu.VMEM((9, n_rows, width), BF),
        dma((4,)),
        dma((2,)),
        dma((3, 12)),
        dma((2, NX, len(SHARES))),
        dma((2, NX)),
        dma((2, NX)),
        dma((2,)),
        dma((3,)),
        dma((3,)),
        dma((2 * NZ,)),
        dma((2 * NZ,)),
        dma((3,)),
        dma((3,)),
        dma((3, 13)),
        dma((9, len(SHARES))),
    ]
    vmem = pl.BlockSpec(memory_space=pltpu.VMEM)
    hbm = pl.BlockSpec(memory_space=pl.ANY)
    return pl.pallas_call(
        kernel,
        out_shape=jax.ShapeDtypeStruct((width, n_rows), BF),
        in_specs=[hbm, hbm, vmem, hbm, vmem],
        out_specs=vmem,
        scratch_shapes=scratch,
        compiler_params=pltpu.CompilerParams(
            collective_id=0, has_side_effects=True, vmem_limit_bytes=56 << 20
        ),
    )(images, ctf_table, group_ids.reshape(1, n_loc), projections, log_prior.reshape(1, n_rows))


def solution(mesh):
    placed = (P("dom", None), P(), P("dom"), P("orient", "dom"), P("orient"))
    return jax.shard_map(
        body, mesh=mesh, in_specs=placed, out_specs=P("dom", "orient"), check_vma=False
    )
```

```python
import functools

import jax
import jax.numpy as jnp
import numpy as np
from jax import lax
from jax.experimental import pallas as pl
from jax.experimental.pallas import tpu as pltpu
from jax.sharding import PartitionSpec as P

BF = jnp.bfloat16
F32 = jnp.float32
MESH = pl.DeviceIdType.MESH
NX, NZ = 4, 8
SHARES = (2, 2, 4, 2, 2, 4)
LOW, HIGH = (0, 1, 2), (3, 4, 5)
PIECES = (0, 1, 2, 3, 4, 5)
MIXED = (0, 3, 1, 4, 2, 5)
LATE = (2, 5, 0, 1, 3, 4)
FOLD = (2, 5)
NQ = 4
PAD = 256
ORDER = ((0, 0), (0, 3), (0, 1), (1, 0), (0, 2), (1, 2), (1, 3), (1, 1))
FAR, DIAG3, DIAG1, OWN3, OWN1, ACROSS, HALF, VIA1, VIA3 = range(9)


def nt(a, b):
    return lax.dot_general(a, b, (((1,), (1,)), ((), ())), preferred_element_type=F32)


def nn(a, b):
    return jnp.dot(a, b, preferred_element_type=F32)


def split3(v):
    a = v.astype(BF)
    r = v - a.astype(F32)
    b = r.astype(BF)
    return a, b, (r - b.astype(F32)).astype(BF)


def kernel(
    images,
    ctf,
    gids,
    proj,
    prior,
    out,
    raw,
    weighted,
    stage,
    blocks,
    ctfv,
    ctf_sq,
    hot,
    hot_t,
    acc,
    norm,
    xsend,
    xrecv,
    stat,
    wts,
    part,
    rx,
    far_raw,
    far_out,
    far,
    wts_far,
    begun,
    final,
    turned,
    out_sem,
    raw_sem,
    loc_sem,
    g_send,
    g_recv,
    w_send,
    w_recv,
    hot_sem,
    x_send,
    x_recv,
    st_send,
    st_recv,
    wt_send,
    wt_recv,
    r_send,
    r_recv,
    f_raw,
    f_send,
    f_recv,
    fy_send,
    wf_send,
    wf_recv,
):
    n_loc, pix = images.shape
    n_rows, width = proj.shape
    step = width // NQ

    def piece(p):
        return pl.ds(sum(SHARES[:p]) * width // 16, SHARES[p] * width // 16)

    scale = float(np.float32(1.0) / np.sqrt(np.float32(pix)))
    dom, ori = lax.axis_index("dom"), lax.axis_index("orient")
    yh, x, core = dom // (2 * NX), lax.rem(dom // 2, NX), lax.rem(dom, 2)
    z, yl = ori // 2, lax.rem(ori, 2)

    def device(yh_, x_, core_, yl_):
        return {"dom": (yh_ * NX + x_) * 2 + core_, "orient": z * 2 + yl_}

    xp = device(yh, lax.rem(x + 1, NX), core, yl)
    xm = device(yh, lax.rem(x + NX - 1, NX), core, yl)
    yp = device(1 - yh, x, core, 1 - yl)
    sib = device(yh, x, 1 - core, yl)
    near = device(yh, x, core, 1 - yl)
    diag = device(yh, x, 1 - core, 1 - yl)
    yd = device(1 - yh, x, 1 - core, 1 - yl)
    fold = SHARES[FOLD[0]] * width // 16

    def peer(k):
        return {"dom": dom, "orient": lax.rem(ori + k, 2 * NZ)}

    def pixel_block(s, j, core_):
        yh_ = yh if s == 0 else 1 - yh
        return (yh_ * NX + lax.rem(x + j, NX)) * 2 + core_

    barrier = pltpu.get_barrier_semaphore()
    for who in (xp, xm, yp, sib, diag, yd):
        pl.semaphore_signal(barrier, inc=1, device_id=who, device_id_type=MESH)

    @pl.loop(1, 2 * NZ)
    def _(k):
        pl.semaphore_signal(barrier, inc=1, device_id=peer(k), device_id_type=MESH)

    jobs = [(s, j, own) for s, j in ORDER for own in (0, 1)]
    n_raw = raw.shape[0]

    def raw_copy(i):
        s, j, own = jobs[i]
        d = pixel_block(s, j, core if own else 1 - core)
        start = pl.multiple_of(d * width, width)
        return pltpu.make_async_copy(
            images.at[:, pl.ds(start, width)], raw.at[i % n_raw], raw_sem.at[i % n_raw]
        )

    ctf_copy = pltpu.make_async_copy(ctf, ctfv, loc_sem.at[1])
    ctf_copy.start()

    def far_start(r):
        d = pixel_block(1, z // 2, core if r == 0 else 1 - core)
        return pl.multiple_of(d * width + width // 4 + lax.rem(z, 2) * (width // 2), fold)

    far_loads = [
        pltpu.make_async_copy(images.at[:, pl.ds(far_start(r), fold)], far_raw.at[r], f_raw.at[r])
        for r in (0, 1)
    ]
    for copy in far_loads:
        copy.start()
    for i in range(n_raw):
        raw_copy(i).start()
    own_copy = pltpu.make_async_copy(proj, blocks.at[0, 0], loc_sem.at[0])
    own_copy.start()

    pl.semaphore_wait(barrier, 6 + 2 * NZ - 1)

    links = (xp, xm, yp)
    counts = [0, 0, 0]
    sent = []

    def gather(link, src, s, j, p):
        copy = pltpu.make_async_remote_copy(
            src_ref=src.at[:, piece(p)],
            dst_ref=blocks.at[s, j, :, piece(p)],
            send_sem=g_send.at[link, counts[link]],
            recv_sem=g_recv.at[s, j, p],
            device_id=links[link],
            device_id_type=MESH,
        )
        counts[link] += 1
        copy.start()
        sent.append(copy)

    def arrived(s, j, p):
        here = blocks.at[s, j, :, piece(p)]
        pltpu.make_async_remote_copy(
            src_ref=here,
            dst_ref=here,
            send_sem=g_send.at[0, 0],
            recv_sem=g_recv.at[s, j, p],
            device_id=xp,
            device_id_type=MESH,
        ).wait_recv()

    for a, b in zip(LOW + HIGH, HIGH + LOW):
        gather(0, proj, 0, 3, a)
        gather(1, proj, 0, 1, b)

    for p in (0, 1):
        gather(2, proj, 1, 0, p)

    group = lax.broadcasted_iota(jnp.int32, (n_rows, n_loc), 0)
    hot_full = jnp.where(group == gids[...], 1.0, 0.0)
    acc[0, 0] = jnp.zeros((n_rows, PAD), F32)
    acc[0, 0, :, :n_loc] = hot_full
    hot_t[...] = jnp.transpose(acc[0, 0])[:n_loc, :].astype(BF)
    twice = jnp.concatenate([acc[0, 0, :8, :], acc[0, 0, :8, :]], axis=0)
    hot[0] = twice.astype(BF)
    hot_copy = pltpu.make_async_remote_copy(
        src_ref=hot.at[0],
        dst_ref=hot.at[1],
        send_sem=hot_sem.at[0],
        recv_sem=hot_sem.at[1],
        device_id=sib,
        device_id_type=MESH,
    )
    hot_copy.start()
    acc[...] = jnp.zeros(acc.shape, F32)
    norm[...] = jnp.zeros(norm.shape, F32)
    ctf_copy.wait()

    half = fold // 2

    def unit(u):
        return pl.ds(u * half, half)

    def far_first(r, u):
        return pltpu.make_async_remote_copy(
            src_ref=far_out.at[r, :, unit(u)],
            dst_ref=far.at[z, 1 - yl, :, unit(u)],
            send_sem=fy_send.at[r, u],
            recv_sem=f_recv.at[0, 0, u],
            device_id=(yp, yd)[r],
            device_id_type=MESH,
        )

    for r in (0, 1):
        far_loads[r].wait()
        rows = nn(hot_t[:, :8], ctfv[:, pl.ds(far_start(r), fold)])
        far_out[r] = (rows * far_raw[r].astype(F32)).astype(BF)

    @pl.when(core == 1 - yl)
    def _():
        for u in (0, 1):
            for r in (0, 1):
                far_first(r, u).start()

    for p in (2, 5, 3, 4):
        gather(2, proj, 1, 0, p)

    around = (peer(2), peer(2 * NZ - 2), near)
    counts_f = [0, 0, 0]

    def far_ref(dz, side, u):
        return far.at[lax.rem(z + dz, NZ), yl if side == 0 else 1 - yl, :, unit(u)]

    def far_on(link, dz, side, u):
        target_dz = (dz + (NZ - 1, 1, 0)[link]) % NZ
        target_side = 1 - side if link == 2 else side
        copy = pltpu.make_async_remote_copy(
            src_ref=far_ref(dz, side, u),
            dst_ref=far_ref(dz, side, u),
            send_sem=f_send.at[link, counts_f[link]],
            recv_sem=f_recv.at[target_side, target_dz, u],
            device_id=around[link],
            device_id_type=MESH,
        )
        counts_f[link] += 1
        copy.start()
        sent.append(copy)

    waited = set()

    def far_in(dz, side, u):
        waited.add((dz, side, u))
        pltpu.make_async_remote_copy(
            src_ref=far_ref(dz, side, u),
            dst_ref=far_ref(dz, side, u),
            send_sem=f_send.at[0, 0],
            recv_sem=f_recv.at[side, dz, u],
            device_id=near,
            device_id_type=MESH,
        ).wait_recv()

    def far_step(dz, side, units=(0, 1), to_near=True):
        for u in units:
            for link, d in ((0, (NZ - dz) % NZ), (1, dz)):
                if dz or link == 0:
                    far_in(d, side, u)
                far_on(link, d, side, u)
                if to_near and (dz or link == 0):
                    far_on(2, d, side, u)

    def weigh(i):
        s, j, own = jobs[i]
        d = pixel_block(s, j, core if own else 1 - core)
        dst = weighted.at[0, s, j] if own else stage.at[s, j]
        raw_copy(i).wait()
        tile = 1024

        @pl.loop(0, width // tile)
        def _(t):
            here = pl.ds(pl.multiple_of(t * tile, tile), tile)
            there = pl.ds(pl.multiple_of(d * width + t * tile, tile), tile)
            table = ctfv[:, there]
            rows = nn(hot_t[:, :8], table)
            dst[:, here] = (rows * raw[i % n_raw, :, here].astype(F32)).astype(BF)
            if own:
                wide = table.astype(F32)
                square = wide * wide
                high = square.astype(BF).astype(F32)
                both = jnp.concatenate([high, square - high], axis=0)
                ctf_sq[s, j, :, here] = both.astype(BF)

        if i + n_raw < len(jobs):
            raw_copy(i + n_raw).start()
        if not own:
            copy = weighted_copy(s, j)
            copy.start()

    def weighted_copy(s, j):
        return pltpu.make_async_remote_copy(
            src_ref=stage.at[s, j],
            dst_ref=weighted.at[1, s, j],
            send_sem=w_send.at[s, j],
            recv_sem=w_recv.at[s, j],
            device_id=sib,
            device_id_type=MESH,
        )

    def score(s, j, here):
        block = blocks[s, j, :, here]
        for nb in (0, 1):
            acc[s, nb, :, :n_loc] += nt(block, weighted[nb, s, j, :, here])
        wide = block.astype(F32)
        square = wide * wide
        high = square.astype(BF)
        low = (square - high.astype(F32)).astype(BF)
        table = ctf_sq[s, j, :, here]
        norm[s] += nt(high, table) + nt(low, table)

    def score_block(s, j):
        @pl.loop(0, NQ)
        def _(q):
            score(s, j, pl.ds(pl.multiple_of(q * step, step), step))

    for i in range(6):
        weigh(i)
    for p in LOW:
        arrived(0, 3, p)
        gather(0, blocks.at[0, 3], 0, 2, p)
    for p in HIGH:
        arrived(0, 1, p)
        gather(1, blocks.at[0, 1], 0, 2, p)
    far_step(0, 0)
    for i in range(6, 11):
        weigh(i)
    far_step(1, 0)
    for i in range(11, 16):
        weigh(i)
    for p in MIXED[:2]:
        arrived(0, 2, p)
        gather(2, blocks.at[0, 2], 1, 2, p)
    for p in LATE:
        arrived(1, 0, p)
        gather(0, blocks.at[1, 0], 1, 3, p)
        gather(1, blocks.at[1, 0], 1, 1, p)
    for p in MIXED[2:4]:
        arrived(0, 2, p)
        gather(2, blocks.at[0, 2], 1, 2, p)
    far_step(2, 0)
    for p in MIXED[4:]:
        arrived(0, 2, p)
        gather(2, blocks.at[0, 2], 1, 2, p)
    for p in HIGH:
        arrived(0, 3, p)
    for p in LOW:
        arrived(0, 1, p)
    own_copy.wait()
    weighted_copy(0, 0).wait_recv()
    score_block(0, 0)
    far_in(NZ - 3, 0, 0)
    far_on(0, NZ - 3, 0, 0)
    far_in(3, 0, 1)
    far_on(1, 3, 0, 1)
    for j in (3, 1, 2):
        weighted_copy(0, j).wait_recv()
        score_block(0, j)

    hot_copy.wait()

    def partial_scores(s, nb):
        a, b, c = split3(norm[s])
        look = nn(a, hot[nb]) + nn(b, hot[nb]) + nn(c, hot[nb])
        return (acc[s, nb] - 0.5 * look) * scale

    def exchange(i, who):
        return pltpu.make_async_remote_copy(
            src_ref=xsend.at[i],
            dst_ref=xrecv.at[i],
            send_sem=x_send.at[i],
            recv_sem=x_recv.at[i],
            device_id=who,
            device_id_type=MESH,
        )

    prior_rows = jnp.transpose(jnp.broadcast_to(prior[...], (n_rows, n_rows)))[:, :1]
    xsend[0] = partial_scores(0, 0) + prior_rows
    xsend[1] = partial_scores(0, 1)
    exchange(0, near).start()
    exchange(1, diag).start()

    far_step(2, 1, units=(0,), to_near=False)
    weighted_copy(1, 0).wait_recv()
    score_block(1, 0)
    for j in (2, 3, 1):
        weighted_copy(1, j).wait_recv()

    def score_far(p):
        arrived(1, 2, p)
        score(1, 2, piece(p))

    def score_late(p):
        for j in (3, 1):
            arrived(1, j, p)
            score(1, j, piece(p))

    score_far(0)
    score_far(3)
    score_late(2)
    score_far(1)
    score_far(4)
    far_step(2, 1, units=(1,), to_near=False)
    score_late(5)
    score_far(2)
    score_late(0)
    score_late(1)
    score_far(5)
    score_late(3)
    score_late(4)

    xsend[2] = partial_scores(1, 1)
    exchange(2, sib).start()
    mine = partial_scores(1, 0)
    exchange(0, near).wait_recv()
    exchange(1, diag).wait_recv()
    mine += xrecv[0] + xrecv[1]
    exchange(2, sib).wait_recv()
    scores = mine + xrecv[2]

    largest = jnp.max(scores, axis=0, keepdims=True)
    expo = jnp.exp(scores - largest)
    stat[0, :, :PAD] = largest
    stat[0, :, PAD:] = jnp.sum(expo, axis=0, keepdims=True)

    def stat_copy(k):
        return pltpu.make_async_remote_copy(
            src_ref=stat.at[0],
            dst_ref=stat.at[k],
            send_sem=st_send.at[k],
            recv_sem=st_recv.at[k],
            device_id=peer(k),
            device_id_type=MESH,
        )

    for k in sorted(range(1, 2 * NZ), key=lambda k: abs(k - NZ)):
        stat_copy(k).start()
    far_in(NZ - 3, 1, 0)
    far_on(0, NZ - 3, 1, 0)
    far_in(3, 1, 1)
    far_on(1, 3, 1, 1)

    @pl.loop(1, 2 * NZ)
    def _(k):
        stat_copy(k).wait_recv()

    top, total = largest, stat[0, :, PAD:]
    for k in range(1, 2 * NZ):
        top = jnp.maximum(top, stat[k, :, :PAD])
    total = jnp.zeros_like(top)
    for k in range(2 * NZ):
        total += stat[k, :, PAD:] * jnp.exp(stat[k, :, :PAD] - top)
    wts[1, 0] = (expo * (jnp.exp(largest - top) / total)).astype(BF)

    def weight_copy(i):
        s, nb, who = ((1, 1, sib), (0, 0, near), (0, 1, diag))[i]
        return pltpu.make_async_remote_copy(
            src_ref=wts.at[1, 0],
            dst_ref=wts.at[s, nb],
            send_sem=wt_send.at[i],
            recv_sem=wt_recv.at[i],
            device_id=who,
            device_id_type=MESH,
        )

    def fold_copy(i):
        return pltpu.make_async_remote_copy(
            src_ref=wts.at[1, 0],
            dst_ref=wts_far.at[core],
            send_sem=wf_send.at[i],
            recv_sem=wf_recv.at[i],
            device_id=(yp, yd)[i],
            device_id_type=MESH,
        )

    def fold_landed(i):
        here = wts_far.at[core if i == 0 else 1 - core]
        pltpu.make_async_remote_copy(
            src_ref=here,
            dst_ref=here,
            send_sem=wf_send.at[i],
            recv_sem=wf_recv.at[i],
            device_id=yp,
            device_id_type=MESH,
        ).wait_recv()

    weight_copy(0).start()
    fold_copy(0).start()
    fold_copy(1).start()
    weight_copy(1).start()
    weight_copy(2).start()

    counts2 = [0, 0, 0]

    def sums(s, j, p):
        total_ = nn(wts[s, 0, :, :n_loc], weighted[0, s, j, :, piece(p)]) + nn(
            wts[s, 1, :, :n_loc], weighted[1, s, j, :, piece(p)]
        )
        if s == 0 and p in FOLD:
            for nb in (0, 1):
                total_ += nn(wts_far[nb, :, :n_loc], far[2 * j + FOLD.index(p), nb])
        return total_

    def landed(kind, p):
        here = rx.at[kind, :, piece(p)]
        pltpu.make_async_remote_copy(
            src_ref=here,
            dst_ref=here,
            send_sem=r_send.at[0, 0],
            recv_sem=r_recv.at[kind, p],
            device_id=xp,
            device_id_type=MESH,
        ).wait_recv()
        return rx[kind, :, piece(p)].astype(F32)

    def scatter(link, kind, s, j, p, *added, begun=None):
        if begun is None:
            total_ = sums(s, j, p)
        else:
            total_ = begun + nn(wts[s, 1, :, :n_loc], weighted[1, s, j, :, piece(p)])
        for k in added:
            total_ = total_ + landed(k, p)
        part[s, j, :, piece(p)] = total_.astype(BF)
        copy = pltpu.make_async_remote_copy(
            src_ref=part.at[s, j, :, piece(p)],
            dst_ref=rx.at[kind, :, piece(p)],
            send_sem=r_send.at[link, counts2[link]],
            recv_sem=r_recv.at[kind, p],
            device_id=links[link],
            device_id_type=MESH,
        )
        counts2[link] += 1
        copy.start()
        sent.append(copy)

    first = [(0, DIAG3, 1, 1, 0), (1, DIAG1, 1, 3, 3)]
    for i, (_, _, s, j, p) in enumerate(first):
        begun[i] = nn(wts[s, 0, :, :n_loc], weighted[0, s, j, :, piece(p)])
    weight_copy(0).wait_recv()
    for i, job in enumerate(first):
        scatter(*job, begun=begun[i])
    scatter(0, DIAG3, 1, 1, 3)
    scatter(1, DIAG1, 1, 3, 0)
    scatter(2, FAR, 1, 2, 3)
    scatter(2, FAR, 1, 2, 0)
    weight_copy(1).wait_recv()
    weight_copy(2).wait_recv()
    scatter(0, OWN3, 0, 1, 0)
    scatter(1, OWN1, 0, 3, 3)
    scatter(2, FAR, 1, 2, 4)
    scatter(2, FAR, 1, 2, 1)
    for side in (0, 1):
        for dz in range(NZ):
            for u in (0, 1):
                if (dz, side, u) not in waited:
                    far_in(dz, side, u)
    fold_landed(0)
    fold_landed(1)
    scatter(0, OWN3, 0, 1, 2)
    scatter(1, OWN1, 0, 3, 5)
    scatter(2, VIA1, 1, 1, 1)
    scatter(2, VIA3, 1, 3, 4)
    scatter(0, HALF, 0, 2, 3, FAR)
    scatter(1, HALF, 0, 2, 0, FAR)
    scatter(2, VIA1, 1, 1, 4)
    scatter(2, VIA3, 1, 3, 1)
    scatter(0, HALF, 0, 2, 5)
    scatter(1, HALF, 0, 2, 2)
    scatter(0, HALF, 0, 2, 4, FAR)
    scatter(1, HALF, 0, 2, 1, FAR)
    scatter(2, ACROSS, 1, 0, 0, DIAG3, DIAG1)
    scatter(2, ACROSS, 1, 0, 3, DIAG3, DIAG1)
    scatter(0, OWN3, 0, 1, 1, VIA1)
    scatter(1, OWN1, 0, 3, 4, VIA3)
    scatter(2, ACROSS, 1, 0, 1)
    scatter(2, ACROSS, 1, 0, 4)
    scatter(0, OWN3, 0, 1, 3, HALF)
    scatter(1, OWN1, 0, 3, 0, HALF)
    scatter(0, OWN3, 0, 1, 5, HALF)
    scatter(1, OWN1, 0, 3, 2, HALF)
    scatter(0, OWN3, 0, 1, 4, HALF, VIA1)
    scatter(1, OWN1, 0, 3, 1, HALF, VIA3)
    for p in PIECES:
        total_ = sums(0, 0, p)
        if p not in FOLD:
            total_ = total_ + landed(ACROSS, p)
        final[:, piece(p)] = total_
    out_copies = []
    for p in (3, 0, 5, 2, 4, 1):
        total_ = final[:, piece(p)] + landed(OWN3, p) + landed(OWN1, p)
        turned[piece(p), :] = jnp.transpose(total_).astype(BF)
        copy = pltpu.make_async_copy(turned.at[piece(p)], out.at[piece(p)], out_sem.at[p])
        copy.start()
        out_copies.append(copy)

    for copy in sent:
        copy.wait_send()
    for s, j in ORDER:
        weighted_copy(s, j).wait_send()
    for i, who in enumerate((near, diag, sib)):
        exchange(i, who).wait_send()

    @pl.loop(1, 2 * NZ)
    def _(k):
        stat_copy(k).wait_send()

    for i in range(3):
        weight_copy(i).wait_send()
    for i in (0, 1):
        fold_copy(i).wait_send()

    @pl.when(core == 1 - yl)
    def _():
        for u in (0, 1):
            for r in (0, 1):
                far_first(r, u).wait_send()

    for copy in out_copies:
        copy.wait()


def body(images, ctf_table, group_ids, projections, log_prior):
    n_loc, pix = images.shape
    n_rows, width = projections.shape
    dma = pltpu.SemaphoreType.DMA
    scratch = [
        pltpu.VMEM((4, n_loc, width), BF),
        pltpu.VMEM((2, 2, NX, n_loc, width), BF),
        pltpu.VMEM((2, NX, n_loc, width), BF),
        pltpu.VMEM((2, NX, n_rows, width), BF),
        pltpu.VMEM(ctf_table.shape, BF),
        pltpu.VMEM((2, NX, 16, width), BF),
        pltpu.VMEM((2, 16, PAD), BF),
        pltpu.VMEM((n_loc, n_rows), BF),
        pltpu.VMEM((2, 2, n_rows, PAD), F32),
        pltpu.VMEM((2, n_rows, 16), F32),
        pltpu.VMEM((3, n_rows, PAD), F32),
        pltpu.VMEM((3, n_rows, PAD), F32),
        pltpu.VMEM((2 * NZ, 1, 2 * PAD), F32),
        pltpu.VMEM((2, 2, n_rows, PAD), BF),
        pltpu.VMEM((2, NX, n_rows, width), BF),
        pltpu.VMEM((9, n_rows, width), BF),
        pltpu.VMEM((2, n_loc, width // 4), BF),
        pltpu.VMEM((2, n_loc, width // 4), BF),
        pltpu.VMEM((NZ, 2, n_loc, width // 4), BF),
        pltpu.VMEM((2, n_rows, PAD), BF),
        pltpu.VMEM((2, n_rows, SHARES[0] * width // 16), F32),
        pltpu.VMEM((n_rows, width), F32),
        pltpu.VMEM((width, n_rows), BF),
        dma((len(SHARES),)),
        dma((4,)),
        dma((2,)),
        dma((3, 15)),
        dma((2, NX, len(SHARES))),
        dma((2, NX)),
        dma((2, NX)),
        dma((2,)),
        dma((3,)),
        dma((3,)),
        dma((2 * NZ,)),
        dma((2 * NZ,)),
        dma((3,)),
        dma((3,)),
        dma((3, 13)),
        dma((9, len(SHARES))),
        dma((2,)),
        dma((3, 10)),
        dma((2, NZ, 2)),
        dma((2, 2)),
        dma((2,)),
        dma((2,)),
    ]
    vmem = pl.BlockSpec(memory_space=pltpu.VMEM)
    hbm = pl.BlockSpec(memory_space=pl.ANY)
    return pl.pallas_call(
        kernel,
        out_shape=jax.ShapeDtypeStruct((width, n_rows), BF),
        in_specs=[hbm, hbm, vmem, hbm, vmem],
        out_specs=hbm,
        scratch_shapes=scratch,
        compiler_params=pltpu.CompilerParams(
            collective_id=0, has_side_effects=True, vmem_limit_bytes=56 << 20
        ),
    )(images, ctf_table, group_ids.reshape(1, n_loc), projections, log_prior.reshape(1, n_rows))


def solution(mesh):
    placed = (P("dom", None), P(), P("dom"), P("orient", "dom"), P("orient"))
    return jax.shard_map(
        body, mesh=mesh, in_specs=placed, out_specs=P("dom", "orient"), check_vma=False
    )
```

```python
import functools

import jax
import jax.numpy as jnp
import numpy as np
from jax import lax
from jax.experimental import pallas as pl
from jax.experimental.pallas import tpu as pltpu
from jax.sharding import PartitionSpec as P

BF = jnp.bfloat16
F32 = jnp.float32
MESH = pl.DeviceIdType.MESH
NX, NZ = 4, 8
SHARES = (4, 4, 4, 2, 2)
LOW, HIGH, VIA = (0, 1), (2, 3, 4), 4
PIECES = (0, 1, 2, 3, 4)
MIXED = (0, 2, 1, 3, 4)
NQ = 4
PAD = 256
ORDER = ((0, 0), (0, 3), (0, 1), (1, 0), (0, 2), (1, 2), (1, 3), (1, 1))
FAR, DIAG3, DIAG1, OWN3, OWN1, ACROSS, HALF, VIA1, VIA3 = range(9)


def nt(a, b):
    return lax.dot_general(a, b, (((1,), (1,)), ((), ())), preferred_element_type=F32)


def nn(a, b):
    return jnp.dot(a, b, preferred_element_type=F32)


def split3(v):
    a = v.astype(BF)
    r = v - a.astype(F32)
    b = r.astype(BF)
    return a, b, (r - b.astype(F32)).astype(BF)


def kernel(
    images,
    ctf,
    gids,
    proj,
    prior,
    out,
    raw,
    weighted,
    stage,
    blocks,
    ctfv,
    ctf_sq,
    hot,
    hot_t,
    acc,
    norm,
    xsend,
    xrecv,
    stat,
    wts,
    part,
    rx,
    begun,
    final,
    turned,
    out_sem,
    raw_sem,
    loc_sem,
    g_send,
    g_recv,
    w_send,
    w_recv,
    hot_sem,
    x_send,
    x_recv,
    st_send,
    st_recv,
    wt_send,
    wt_recv,
    r_send,
    r_recv,
):
    n_loc, pix = images.shape
    n_rows, width = proj.shape
    step = width // NQ

    def piece(p):
        return pl.ds(sum(SHARES[:p]) * width // 16, SHARES[p] * width // 16)

    scale = float(np.float32(1.0) / np.sqrt(np.float32(pix)))
    dom, ori = lax.axis_index("dom"), lax.axis_index("orient")
    yh, x, core = dom // (2 * NX), lax.rem(dom // 2, NX), lax.rem(dom, 2)
    z, yl = ori // 2, lax.rem(ori, 2)

    def device(yh_, x_, core_, yl_):
        return {"dom": (yh_ * NX + x_) * 2 + core_, "orient": z * 2 + yl_}

    xp = device(yh, lax.rem(x + 1, NX), core, yl)
    xm = device(yh, lax.rem(x + NX - 1, NX), core, yl)
    yp = device(1 - yh, x, core, 1 - yl)
    sib = device(yh, x, 1 - core, yl)
    near = device(yh, x, core, 1 - yl)
    diag = device(yh, x, 1 - core, 1 - yl)

    def peer(k):
        return {"dom": dom, "orient": lax.rem(ori + k, 2 * NZ)}

    def pixel_block(s, j, core_):
        yh_ = yh if s == 0 else 1 - yh
        return (yh_ * NX + lax.rem(x + j, NX)) * 2 + core_

    barrier = pltpu.get_barrier_semaphore()
    for who in (xp, xm, yp, sib, diag):
        pl.semaphore_signal(barrier, inc=1, device_id=who, device_id_type=MESH)

    @pl.loop(1, 2 * NZ)
    def _(k):
        pl.semaphore_signal(barrier, inc=1, device_id=peer(k), device_id_type=MESH)

    jobs = [(s, j, own) for s, j in ORDER for own in (0, 1)]
    n_raw = raw.shape[0]

    def raw_copy(i):
        s, j, own = jobs[i]
        d = pixel_block(s, j, core if own else 1 - core)
        start = pl.multiple_of(d * width, width)
        return pltpu.make_async_copy(
            images.at[:, pl.ds(start, width)], raw.at[i % n_raw], raw_sem.at[i % n_raw]
        )

    ctf_copy = pltpu.make_async_copy(ctf, ctfv, loc_sem.at[1])
    ctf_copy.start()
    for i in range(n_raw):
        raw_copy(i).start()
    own_copy = pltpu.make_async_copy(proj, blocks.at[0, 0], loc_sem.at[0])
    own_copy.start()

    pl.semaphore_wait(barrier, 5 + 2 * NZ - 1)

    links = (xp, xm, yp)
    counts = [0, 0, 0]
    sent = []

    def gather(link, src, s, j, p):
        copy = pltpu.make_async_remote_copy(
            src_ref=src.at[:, piece(p)],
            dst_ref=blocks.at[s, j, :, piece(p)],
            send_sem=g_send.at[link, counts[link]],
            recv_sem=g_recv.at[s, j, p],
            device_id=links[link],
            device_id_type=MESH,
        )
        counts[link] += 1
        copy.start()
        sent.append(copy)

    def arrived(s, j, p):
        here = blocks.at[s, j, :, piece(p)]
        pltpu.make_async_remote_copy(
            src_ref=here,
            dst_ref=here,
            send_sem=g_send.at[0, 0],
            recv_sem=g_recv.at[s, j, p],
            device_id=xp,
            device_id_type=MESH,
        ).wait_recv()

    for a, b in zip(LOW + HIGH, HIGH + LOW):
        gather(0, proj, 0, 3, a)
        gather(1, proj, 0, 1, b)
        gather(2, proj, 1, 0, a)

    group = lax.broadcasted_iota(jnp.int32, (n_rows, n_loc), 0)
    hot_full = jnp.where(group == gids[...], 1.0, 0.0)
    acc[0, 0] = jnp.zeros((n_rows, PAD), F32)
    acc[0, 0, :, :n_loc] = hot_full
    hot_t[...] = jnp.transpose(acc[0, 0])[:n_loc, :].astype(BF)
    twice = jnp.concatenate([acc[0, 0, :8, :], acc[0, 0, :8, :]], axis=0)
    hot[0] = twice.astype(BF)
    hot_copy = pltpu.make_async_remote_copy(
        src_ref=hot.at[0],
        dst_ref=hot.at[1],
        send_sem=hot_sem.at[0],
        recv_sem=hot_sem.at[1],
        device_id=sib,
        device_id_type=MESH,
    )
    hot_copy.start()
    acc[...] = jnp.zeros(acc.shape, F32)
    norm[...] = jnp.zeros(norm.shape, F32)
    ctf_copy.wait()

    def weigh(i):
        s, j, own = jobs[i]
        d = pixel_block(s, j, core if own else 1 - core)
        dst = weighted.at[0, s, j] if own else stage.at[s, j]
        raw_copy(i).wait()
        tile = 1024

        @pl.loop(0, width // tile)
        def _(t):
            here = pl.ds(pl.multiple_of(t * tile, tile), tile)
            there = pl.ds(pl.multiple_of(d * width + t * tile, tile), tile)
            table = ctfv[:, there]
            rows = nn(hot_t[:, :8], table)
            dst[:, here] = (rows * raw[i % n_raw, :, here].astype(F32)).astype(BF)
            if own:
                wide = table.astype(F32)
                square = wide * wide
                high = square.astype(BF).astype(F32)
                both = jnp.concatenate([high, square - high], axis=0)
                ctf_sq[s, j, :, here] = both.astype(BF)

        if i + n_raw < len(jobs):
            raw_copy(i + n_raw).start()
        if not own:
            copy = weighted_copy(s, j)
            copy.start()

    def weighted_copy(s, j):
        return pltpu.make_async_remote_copy(
            src_ref=stage.at[s, j],
            dst_ref=weighted.at[1, s, j],
            send_sem=w_send.at[s, j],
            recv_sem=w_recv.at[s, j],
            device_id=sib,
            device_id_type=MESH,
        )

    def score(s, j, here):
        block = blocks[s, j, :, here]
        for nb in (0, 1):
            acc[s, nb, :, :n_loc] += nt(block, weighted[nb, s, j, :, here])
        wide = block.astype(F32)
        square = wide * wide
        high = square.astype(BF)
        low = (square - high.astype(F32)).astype(BF)
        table = ctf_sq[s, j, :, here]
        norm[s] += nt(high, table) + nt(low, table)

    def score_block(s, j):
        @pl.loop(0, NQ)
        def _(q):
            score(s, j, pl.ds(pl.multiple_of(q * step, step), step))

    for i in range(8):
        weigh(i)
    for p in LOW:
        arrived(0, 3, p)
        gather(0, blocks.at[0, 3], 0, 2, p)
    for p in HIGH:
        arrived(0, 1, p)
        gather(1, blocks.at[0, 1], 0, 2, p)
    for i in range(8, 16):
        weigh(i)
    gather(2, blocks.at[0, 1], 1, 1, VIA)
    for p in PIECES:
        arrived(1, 0, p)
        if p != VIA:
            gather(0, blocks.at[1, 0], 1, 3, p)
            gather(1, blocks.at[1, 0], 1, 1, p)
    for p in HIGH:
        arrived(0, 3, p)
    gather(2, blocks.at[0, 3], 1, 3, VIA)
    for p in LOW:
        arrived(0, 1, p)
    own_copy.wait()
    weighted_copy(0, 0).wait_recv()
    score_block(0, 0)
    for p in MIXED[:2]:
        arrived(0, 2, p)
        gather(2, blocks.at[0, 2], 1, 2, p)
    weighted_copy(0, 3).wait_recv()
    score_block(0, 3)
    for p in MIXED[2:]:
        arrived(0, 2, p)
        gather(2, blocks.at[0, 2], 1, 2, p)
    weighted_copy(0, 1).wait_recv()
    score_block(0, 1)
    weighted_copy(0, 2).wait_recv()
    score_block(0, 2)

    hot_copy.wait()

    def partial_scores(s, nb):
        a, b, c = split3(norm[s])
        look = nn(a, hot[nb]) + nn(b, hot[nb]) + nn(c, hot[nb])
        return (acc[s, nb] - 0.5 * look) * scale

    def exchange(i, who):
        return pltpu.make_async_remote_copy(
            src_ref=xsend.at[i],
            dst_ref=xrecv.at[i],
            send_sem=x_send.at[i],
            recv_sem=x_recv.at[i],
            device_id=who,
            device_id_type=MESH,
        )

    prior_rows = jnp.transpose(jnp.broadcast_to(prior[...], (n_rows, n_rows)))[:, :1]
    xsend[0] = partial_scores(0, 0) + prior_rows
    xsend[1] = partial_scores(0, 1)
    exchange(0, near).start()
    exchange(1, diag).start()

    weighted_copy(1, 0).wait_recv()
    score_block(1, 0)
    for j in (2, 3, 1):
        weighted_copy(1, j).wait_recv()
    arrived(1, 1, VIA)
    score(1, 1, piece(VIA))
    arrived(1, 3, VIA)
    score(1, 3, piece(VIA))
    for a, p in zip(MIXED, PIECES):
        if p != VIA:
            arrived(1, 3, p)
            score(1, 3, piece(p))
            arrived(1, 1, p)
            score(1, 1, piece(p))
        arrived(1, 2, a)
        score(1, 2, piece(a))

    xsend[2] = partial_scores(1, 1)
    exchange(2, sib).start()
    mine = partial_scores(1, 0)
    exchange(0, near).wait_recv()
    exchange(1, diag).wait_recv()
    mine += xrecv[0] + xrecv[1]
    exchange(2, sib).wait_recv()
    scores = mine + xrecv[2]

    largest = jnp.max(scores, axis=0, keepdims=True)
    expo = jnp.exp(scores - largest)
    stat[0, :, :PAD] = largest
    stat[0, :, PAD:] = jnp.sum(expo, axis=0, keepdims=True)

    def stat_copy(k):
        return pltpu.make_async_remote_copy(
            src_ref=stat.at[0],
            dst_ref=stat.at[k],
            send_sem=st_send.at[k],
            recv_sem=st_recv.at[k],
            device_id=peer(k),
            device_id_type=MESH,
        )

    for k in sorted(range(1, 2 * NZ), key=lambda k: abs(k - NZ)):
        stat_copy(k).start()

    @pl.loop(1, 2 * NZ)
    def _(k):
        stat_copy(k).wait_recv()

    top, total = largest, stat[0, :, PAD:]
    for k in range(1, 2 * NZ):
        top = jnp.maximum(top, stat[k, :, :PAD])
    total = jnp.zeros_like(top)
    for k in range(2 * NZ):
        total += stat[k, :, PAD:] * jnp.exp(stat[k, :, :PAD] - top)
    wts[1, 0] = (expo * (jnp.exp(largest - top) / total)).astype(BF)

    def weight_copy(i):
        s, nb, who = ((1, 1, sib), (0, 0, near), (0, 1, diag))[i]
        return pltpu.make_async_remote_copy(
            src_ref=wts.at[1, 0],
            dst_ref=wts.at[s, nb],
            send_sem=wt_send.at[i],
            recv_sem=wt_recv.at[i],
            device_id=who,
            device_id_type=MESH,
        )

    for i in range(3):
        weight_copy(i).start()

    counts2 = [0, 0, 0]

    def sums(s, j, p):
        return nn(wts[s, 0, :, :n_loc], weighted[0, s, j, :, piece(p)]) + nn(
            wts[s, 1, :, :n_loc], weighted[1, s, j, :, piece(p)]
        )

    def landed(kind, p):
        here = rx.at[kind, :, piece(p)]
        pltpu.make_async_remote_copy(
            src_ref=here,
            dst_ref=here,
            send_sem=r_send.at[0, 0],
            recv_sem=r_recv.at[kind, p],
            device_id=xp,
            device_id_type=MESH,
        ).wait_recv()
        return rx[kind, :, piece(p)].astype(F32)

    def scatter(link, kind, s, j, p, *added, begun=None):
        if begun is None:
            total_ = sums(s, j, p)
        else:
            total_ = begun + nn(wts[s, 1, :, :n_loc], weighted[1, s, j, :, piece(p)])
        for k in added:
            total_ = total_ + landed(k, p)
        part[s, j, :, piece(p)] = total_.astype(BF)
        copy = pltpu.make_async_remote_copy(
            src_ref=part.at[s, j, :, piece(p)],
            dst_ref=rx.at[kind, :, piece(p)],
            send_sem=r_send.at[link, counts2[link]],
            recv_sem=r_recv.at[kind, p],
            device_id=links[link],
            device_id_type=MESH,
        )
        counts2[link] += 1
        copy.start()
        sent.append(copy)

    first = [(0, DIAG3, 1, 1, 0), (1, DIAG1, 1, 3, 0), (2, FAR, 1, 2, 0)]
    for i, (_, _, s, j, p) in enumerate(first):
        begun[i] = nn(wts[s, 0, :, :n_loc], weighted[0, s, j, :, piece(p)])
    weight_copy(0).wait_recv()
    for i, job in enumerate(first):
        scatter(*job, begun=begun[i])
    for a, p in zip(MIXED[1:], PIECES[1:]):
        if p != VIA:
            scatter(0, DIAG3, 1, 1, p)
            scatter(1, DIAG1, 1, 3, p)
        scatter(2, FAR, 1, 2, a)
    scatter(2, VIA3, 1, 3, VIA)
    scatter(2, VIA1, 1, 1, VIA)
    weight_copy(1).wait_recv()
    weight_copy(2).wait_recv()
    scatter(1, HALF, 0, 2, 0, FAR)
    scatter(2, ACROSS, 1, 0, 0, DIAG3, DIAG1)
    scatter(0, HALF, 0, 2, 2, FAR)
    scatter(2, ACROSS, 1, 0, 1, DIAG3, DIAG1)
    scatter(1, HALF, 0, 2, 1, FAR)
    scatter(2, ACROSS, 1, 0, 2, DIAG3, DIAG1)
    scatter(0, HALF, 0, 2, 3, FAR)
    scatter(2, ACROSS, 1, 0, 3, DIAG3, DIAG1)
    scatter(2, ACROSS, 1, 0, 4)
    scatter(0, HALF, 0, 2, 4, FAR)
    scatter(0, OWN3, 0, 1, 0)
    scatter(1, OWN1, 0, 3, 2)
    scatter(0, OWN3, 0, 1, 1)
    scatter(1, OWN1, 0, 3, 3)
    scatter(1, OWN1, 0, 3, 4, VIA3)
    scatter(1, OWN1, 0, 3, 0, HALF)
    scatter(0, OWN3, 0, 1, 2, HALF)
    scatter(1, OWN1, 0, 3, 1, HALF)
    scatter(0, OWN3, 0, 1, 3, HALF)
    scatter(0, OWN3, 0, 1, 4, HALF, VIA1)
    for p in PIECES:
        final[:, piece(p)] = sums(0, 0, p) + landed(ACROSS, p)
    out_copies = []
    for p in (2, 0, 3, 1, 4):
        total_ = final[:, piece(p)] + landed(OWN3, p) + landed(OWN1, p)
        turned[piece(p), :] = jnp.transpose(total_).astype(BF)
        copy = pltpu.make_async_copy(turned.at[piece(p)], out.at[piece(p)], out_sem.at[p])
        copy.start()
        out_copies.append(copy)

    for copy in sent:
        copy.wait_send()
    for s, j in ORDER:
        weighted_copy(s, j).wait_send()
    for i, who in enumerate((near, diag, sib)):
        exchange(i, who).wait_send()

    @pl.loop(1, 2 * NZ)
    def _(k):
        stat_copy(k).wait_send()

    for i in range(3):
        weight_copy(i).wait_send()
    for copy in out_copies:
        copy.wait()


def body(images, ctf_table, group_ids, projections, log_prior):
    n_loc, pix = images.shape
    n_rows, width = projections.shape
    dma = pltpu.SemaphoreType.DMA
    scratch = [
        pltpu.VMEM((4, n_loc, width), BF),
        pltpu.VMEM((2, 2, NX, n_loc, width), BF),
        pltpu.VMEM((2, NX, n_loc, width), BF),
        pltpu.VMEM((2, NX, n_rows, width), BF),
        pltpu.VMEM(ctf_table.shape, BF),
        pltpu.VMEM((2, NX, 16, width), BF),
        pltpu.VMEM((2, 16, PAD), BF),
        pltpu.VMEM((n_loc, n_rows), BF),
        pltpu.VMEM((2, 2, n_rows, PAD), F32),
        pltpu.VMEM((2, n_rows, 16), F32),
        pltpu.VMEM((3, n_rows, PAD), F32),
        pltpu.VMEM((3, n_rows, PAD), F32),
        pltpu.VMEM((2 * NZ, 1, 2 * PAD), F32),
        pltpu.VMEM((2, 2, n_rows, PAD), BF),
        pltpu.VMEM((2, NX, n_rows, width), BF),
        pltpu.VMEM((9, n_rows, width), BF),
        pltpu.VMEM((3, n_rows, SHARES[0] * width // 16), F32),
        pltpu.VMEM((n_rows, width), F32),
        pltpu.VMEM((width, n_rows), BF),
        dma((len(SHARES),)),
        dma((4,)),
        dma((2,)),
        dma((3, 12)),
        dma((2, NX, len(SHARES))),
        dma((2, NX)),
        dma((2, NX)),
        dma((2,)),
        dma((3,)),
        dma((3,)),
        dma((2 * NZ,)),
        dma((2 * NZ,)),
        dma((3,)),
        dma((3,)),
        dma((3, 13)),
        dma((9, len(SHARES))),
    ]
    vmem = pl.BlockSpec(memory_space=pltpu.VMEM)
    hbm = pl.BlockSpec(memory_space=pl.ANY)
    return pl.pallas_call(
        kernel,
        out_shape=jax.ShapeDtypeStruct((width, n_rows), BF),
        in_specs=[hbm, hbm, vmem, hbm, vmem],
        out_specs=hbm,
        scratch_shapes=scratch,
        compiler_params=pltpu.CompilerParams(
            collective_id=0, has_side_effects=True, vmem_limit_bytes=56 << 20
        ),
    )(images, ctf_table, group_ids.reshape(1, n_loc), projections, log_prior.reshape(1, n_rows))


def solution(mesh):
    placed = (P("dom", None), P(), P("dom"), P("orient", "dom"), P("orient"))
    return jax.shard_map(
        body, mesh=mesh, in_specs=placed, out_specs=P("dom", "orient"), check_vma=False
    )
```
